32 devices in a mesh: feat: 8 (over y, x, core), node: 4 (over z).
Axes of the slice: x: 2, y: 2, z: 4, core: 2. Of those that a mesh axis runs over, the one named last changes fastest.
Arguments:
- features: bfloat16 [4, 512, 16384], P('node', 'feat'), may hold values from -6 to 6
- target_ids: int32 [4, 4096], P('node'), may hold values from 0 to 16383
- block_ids: int32 [4, 32, 8], P('node'), may hold values from 0 to 127
- tile_counts: int32 [4, 32], P('node'), may hold values from 1 to 8, as said below
- adjacency: bfloat16 [4, 32, 8, 128, 128], P('node'), may hold values from 0 to 0.25
- w_neigh: bfloat16 [256, 512], P(None, 'feat'), may hold values from -0.1875 to 0.1875
- w_self: bfloat16 [256, 512], P(None, 'feat'), may hold values from -0.1875 to 0.1875
- w_head: bfloat16 [256, 256], replicated, may hold values from -0.375 to 0.375
- grad_scores: bfloat16 [4, 4096, 256], P('node', 'feat'), may hold values from -6 to 6
Outputs:
- scores: bfloat16 [4, 4096, 256], P('node', 'feat')
- grad_head: float32 [256, 256], replicated
- grad_neigh: float32 [256, 512], P(None, 'feat')
- grad_self: float32 [256, 512], P(None, 'feat')
The draws below stay inside these ranges and needn't reach their ends.
Inputs may be any that keep to these rules, and one draw needn't show every extreme that they name: `tile_counts`: one group, drawn from the seed, has all of its tiles at 8 live slots; every tile of the other groups has fewer than 8.
All inputs are finite; a program needn't handle non-finite values.
Results may differ from the reference program's by a relative error of at most 0.0056.
Values may be sent and summed in bfloat16 or wider, within the bound.
A program may use at most 64 MiB of HBM per device.

```python
import jax
import jax.numpy as jnp

F = 512
HID = 256
OUT = 256
MAXT = 8
TT = 32
SB = 128
TGT_N = 4096
SRC = 16384
N_NODE = 4


def draw_tile_counts(key, part):
    first_key, second_key = jax.random.split(key, 2)
    hottest = jax.random.randint(first_key, (), 0, N_NODE)
    light_counts = jax.random.randint(second_key, (N_NODE, TT), 1, MAXT)
    heavy_rows = jnp.arange(N_NODE, dtype=jnp.int32)[:, None] == hottest
    counts_all = jnp.where(heavy_rows, MAXT, light_counts)
    return counts_all.astype(jnp.int32)


def plant(drawn, rng, smallest, high):
    index_at = [jax.random.randint(jax.random.fold_in(rng, axis), (), 0, length) for axis, length in enumerate(drawn.shape)]
    main_axis = drawn.shape.index(max(drawn.shape))
    next_to = index_at[:main_axis] + [(index_at[main_axis] + 1) % drawn.shape[main_axis]] + index_at[main_axis + 1:]
    return drawn.at[tuple(index_at)].set(smallest).at[tuple(next_to)].set(high)


def shard_levels(stream_key, dims, cuts, least, largest):
    loudness, own = 1.0, jax.random.fold_in(stream_key, 6)
    for position, shards_of in cuts:
        heights = jnp.exp(jax.random.uniform(jax.random.fold_in(own, position), (shards_of,), jnp.float32, least / len(cuts), largest / len(cuts)))
        loudness = loudness * jnp.repeat(heights, dims[position] // shards_of).reshape([-1 if axis == position else 1 for axis in range(len(dims))])
    return loudness


def normal_values(key, extent, scale, limit, cuts=(), held_as=jnp.bfloat16):
    result = jax.random.normal(key, extent, jnp.float32) * scale
    if len(cuts) > 0:
        result = shard_levels(key, extent, cuts, -0.22, 0.18) * result
    return jnp.clip(result, min=-limit, max=limit).astype(held_as)


def setup_inputs(seed: int = 0) -> dict:
    seeds = jax.random.split(jax.random.key(seed), 10)
    features = normal_values(seeds[0], (N_NODE, F, SRC), 1.0, 6.0, ((0, 4), (1, 8)))
    target_ids = plant(jax.random.randint(seeds[1], (N_NODE, TGT_N), 0, SRC), jax.random.fold_in(seeds[1], 1), 0, SRC - 1).astype(jnp.int32)
    block_ids = plant(jax.random.randint(seeds[2], (N_NODE, TT, MAXT), 0, SB), jax.random.fold_in(seeds[2], 1), 0, SB - 1).astype(jnp.int32)
    tile_counts = draw_tile_counts(jax.random.fold_in(seeds[9], 71), 0)
    adjacency = jnp.clip(0.25 * jax.random.uniform(seeds[4], (N_NODE, TT, MAXT, 128, 128), jnp.float32) ** shard_levels(seeds[4], (N_NODE, TT, MAXT, 128, 128), ((0, 4),), -0.2, 0.2), 0.0, 0.25).astype(jnp.bfloat16)
    w_neigh = normal_values(seeds[5], (HID, F), (2 * F) ** -0.5, 0.1875, ((1, 8),))
    w_self = normal_values(seeds[6], (HID, F), (2 * F) ** -0.5, 0.1875, ((1, 8),))
    w_head = normal_values(seeds[7], (OUT, HID), HID ** -0.5, 0.375)
    grad_scores = normal_values(seeds[8], (N_NODE, TGT_N, OUT), 1.0, 6.0, ((0, 4), (1, 8)))
    return dict(features=features, target_ids=target_ids, block_ids=block_ids, tile_counts=tile_counts, adjacency=adjacency, w_neigh=w_neigh, w_self=w_self, w_head=w_head, grad_scores=grad_scores)


def aggregate_group(feature_rows, block_row, count_row, adjacency_group):
    width = feature_rows.shape[0]
    blocks = feature_rows.reshape(width, SB, 128)
    gathered = jnp.take(blocks, block_row.reshape(-1), axis=1).reshape(width, TT, MAXT, 128)
    live = (jnp.arange(MAXT, dtype=jnp.int32)[None, :] < count_row[:, None]).astype(jnp.float32)
    masked = gathered.astype(jnp.float32) * live[None, :, :, None]
    summed = jnp.einsum("tkrs,ftks->ftr", adjacency_group.astype(jnp.float32), masked)
    summed = summed / count_row.astype(jnp.float32)[None, :, None]
    return summed.astype(jnp.bfloat16).reshape(width, TT * 128)


def reference(features, target_ids, block_ids, tile_counts, adjacency, w_neigh, w_self, w_head, grad_scores):
    grad_head = jnp.zeros((OUT, HID), jnp.float32)
    grad_neigh = jnp.zeros((HID, F), jnp.float32)
    grad_self = jnp.zeros((HID, F), jnp.float32)
    score_list = []
    for group_index in range(N_NODE):
        aggregate = aggregate_group(features[group_index], block_ids[group_index], tile_counts[group_index], adjacency[group_index])
        own = jnp.take(features[group_index], target_ids[group_index], axis=1)
        preact = jnp.dot(aggregate.T, w_neigh.T, preferred_element_type=jnp.float32) + jnp.dot(own.T, w_self.T, preferred_element_type=jnp.float32)
        hidden = jax.nn.silu(preact).astype(jnp.bfloat16)
        score_list.append(jnp.dot(hidden, w_head.T, preferred_element_type=jnp.float32).astype(jnp.bfloat16))
        cotangent = grad_scores[group_index]
        grad_head = grad_head + jnp.dot(cotangent.T, hidden, preferred_element_type=jnp.float32)
        grad_hidden = jnp.dot(cotangent, w_head, preferred_element_type=jnp.float32)
        sigma = jax.nn.sigmoid(preact)
        grad_pre = (grad_hidden * sigma * (1.0 + preact * (1.0 - sigma))).astype(jnp.bfloat16)
        grad_neigh = grad_neigh + jnp.dot(grad_pre.T, aggregate.T, preferred_element_type=jnp.float32)
        grad_self = grad_self + jnp.dot(grad_pre.T, own.T, preferred_element_type=jnp.float32)
    scores = jnp.stack(score_list, axis=0)
    return (scores, grad_head, grad_neigh, grad_self)
```

```python
import functools

import jax
import jax.numpy as jnp
from jax import lax
from jax.experimental import pallas as pl
from jax.experimental.pallas import tpu as pltpu
from jax.sharding import PartitionSpec as P

F32 = jnp.float32
BF16 = jnp.bfloat16
VMEM_BYTES = 56 * 1024 * 1024


def nn(left, right):
    return lax.dot_general(left, right, (((1,), (0,)), ((), ())), preferred_element_type=F32)


def nt(left, right):
    return lax.dot_general(left, right, (((1,), (1,)), ((), ())), preferred_element_type=F32)


def gather_kernel(
    ids_ref, blocks_ref, counts_ref, feat_ref, wn_ref, ws_ref, own_ref, near_ref, wt_ref, table, rows
):
    width, sources = feat_ref.shape
    parts, _, targets = own_ref.shape
    wt_ref[:width, :] = wn_ref[...].astype(F32).T.astype(BF16)
    wt_ref[width:, :] = ws_ref[...].astype(F32).T.astype(BF16)

    def fill(step, carry):
        for piece in range(4):
            at = pl.multiple_of((step * 4 + piece) * 128, 128)
            table[pl.ds(at, 128), :] = feat_ref[:, pl.ds(at, 128)].astype(F32).T
        return carry

    lax.fori_loop(0, sources // 512, fill, 0)

    tiles = near_ref.shape[0]
    slots = near_ref.shape[2] // 128

    def neighbours(tile, carry):
        count = counts_ref[tile]
        for slot in range(slots):
            at = pl.multiple_of(blocks_ref[tile * slots + slot] * 128, 128)
            live = jnp.full((width, 128), (slot < count).astype(F32), F32).astype(BF16)
            near_ref[tile, :, slot * 128 : slot * 128 + 128] = feat_ref[:, pl.ds(at, 128)] * live
        return carry

    lax.fori_loop(0, tiles, neighbours, 0)

    def chunk(step, carry):
        base = step * 128
        for row in range(128):
            rows[row : row + 1, :] = table[pl.ds(ids_ref[base + row], 1), :]
        part = base // targets
        inside = pl.multiple_of(base - part * targets, 128)
        own_ref[part, :, pl.ds(inside, 128)] = rows[...].T.astype(BF16)
        return carry

    lax.fori_loop(0, parts * targets // 128, chunk, 0)


def gather_own(ids, blocks, counts, feat, w_neigh, w_self, parts):
    width, sources = feat.shape
    hid = w_neigh.shape[0]
    targets = ids.shape[0] // parts
    tiles, slots = counts.shape[0], blocks.shape[0] // counts.shape[0]
    vmem = pl.BlockSpec(memory_space=pltpu.VMEM)
    smem = pl.BlockSpec(memory_space=pltpu.SMEM)
    return pl.pallas_call(
        gather_kernel,
        out_shape=(
            jax.ShapeDtypeStruct((parts, width, targets), BF16),
            jax.ShapeDtypeStruct((tiles, width, slots * 128), BF16),
            jax.ShapeDtypeStruct((2 * width, hid), BF16),
        ),
        in_specs=[smem, smem, smem, vmem, vmem, vmem],
        out_specs=(vmem, vmem, vmem),
        scratch_shapes=[pltpu.VMEM((sources, width), F32), pltpu.VMEM((128, width), F32)],
        compiler_params=pltpu.CompilerParams(vmem_limit_bytes=VMEM_BYTES),
        name="own_gather",
    )(ids, blocks, counts, feat, w_neigh, w_self)


def main_kernel(
    parts, nodes, counts_ref, near_ref, adj_ref, own_ref, wt_ref, wh_ref, gs_ref,
    scores_ref, grads_ref, head_ref,
    x_all, w_all, agg_send, head_part, head_recv, head_node, head_all,
    g_part, g_send, g_recv, g_node,
    w_sems, own_sems, agg_sems, hrs_sems, grs_sems, hn_sems, gn_sems, hag_sems,
):
    me = lax.axis_index("feat")
    my_node = lax.axis_index("node")
    width = near_ref.shape[1]
    tiles, slots = adj_ref.shape[:2]
    per_part = tiles // parts
    hid = wh_ref.shape[1]
    targets = gs_ref.shape[0]

    def feat_copy(step, src, dst, sems):
        peer = lax.rem(me + step, parts)
        return pltpu.make_async_remote_copy(
            src_ref=src, dst_ref=dst, send_sem=sems.at[0, step], recv_sem=sems.at[1, step],
            device_id={"feat": peer}, device_id_type=pl.DeviceIdType.MESH,
        )

    def node_copy(step, src, dst, sems):
        peer = lax.rem(my_node + step, nodes)
        return pltpu.make_async_remote_copy(
            src_ref=src, dst_ref=dst, send_sem=sems.at[0, step], recv_sem=sems.at[1, step],
            device_id={"node": peer}, device_id_type=pl.DeviceIdType.MESH,
        )

    barrier = pltpu.get_barrier_semaphore()
    for step in range(1, parts):
        pl.semaphore_signal(
            barrier, inc=1, device_id={"feat": lax.rem(me + step, parts)},
            device_id_type=pl.DeviceIdType.MESH,
        )
    for step in range(1, nodes):
        pl.semaphore_signal(
            barrier, inc=1, device_id={"node": lax.rem(my_node + step, nodes)},
            device_id_type=pl.DeviceIdType.MESH,
        )
    pl.semaphore_wait(barrier, parts + nodes - 2)

    w_copies, own_copies, agg_copies = [], [], []
    for step in range(1, parts):
        peer = lax.rem(me + step, parts)
        copy = feat_copy(step, own_ref.at[peer], x_all.at[me, pl.ds(width, width)], own_sems)
        copy.start()
        own_copies.append(copy)
        copy = feat_copy(step, wt_ref, w_all.at[me], w_sems)
        copy.start()
        w_copies.append(copy)

    def aggregate(tile):
        edges = jnp.concatenate([adj_ref[tile, slot] for slot in range(slots)], axis=1)
        total = nt(near_ref[tile], edges)
        return (total / jnp.full(total.shape, counts_ref[tile], F32)).astype(BF16)

    for step in range(1, parts + 1):
        peer = lax.rem(me + step, parts)
        for tile in range(per_part):
            part = aggregate(peer * per_part + tile)
            if step < parts:
                agg_send[step, :, tile * 128 : tile * 128 + 128] = part
            else:
                x_all[me, :width, tile * 128 : tile * 128 + 128] = part
        if step < parts:
            copy = feat_copy(step, agg_send.at[step], x_all.at[me, pl.ds(0, width)], agg_sems)
            copy.start()
            agg_copies.append(copy)
    x_all[me, width:, :] = own_ref[me]
    w_all[me] = wt_ref[...]

    grad_t = gs_ref[...].astype(F32).T.astype(BF16)
    head_t = wh_ref[...].astype(F32).T.astype(BF16)
    grad_hidden = nn(head_t, grad_t)

    for copy in w_copies:
        copy.wait_recv()
    weights = w_all[...].reshape(parts * 2 * width, hid).astype(F32).T.astype(BF16)
    for copy in own_copies:
        copy.wait_recv()
    for copy in agg_copies:
        copy.wait_recv()
    x = x_all[...].reshape(parts * 2 * width, targets)
    preact = nn(weights, x)
    sigma = 1.0 / (1.0 + jnp.exp(-preact))
    hidden = (preact * sigma).astype(BF16)
    head_part[...] = nt(grad_t, hidden).reshape(head_part.shape)
    hrs = []
    for step in range(1, parts):
        peer = lax.rem(me + step, parts)
        copy = feat_copy(step, head_part.at[peer], head_recv.at[step], hrs_sems)
        copy.start()
        hrs.append(copy)
    grad_pre = (grad_hidden * sigma * (1.0 + preact * (1.0 - sigma))).astype(BF16)
    grads = nt(x, grad_pre).reshape(g_part.shape)
    g_part[...] = grads
    g_send[...] = grads.astype(BF16)
    grs = []
    for step in range(1, parts):
        peer = lax.rem(me + step, parts)
        copy = feat_copy(step, g_send.at[peer], g_recv.at[step], grs_sems)
        copy.start()
        grs.append(copy)
    scores_ref[...] = nn(wh_ref[...], hidden).T.astype(BF16)

    total = head_part[me]
    for step, copy in enumerate(hrs, 1):
        copy.wait_recv()
        total += head_recv[step]
    head_node[my_node] = total
    hns = []
    for step in range(1, nodes):
        copy = node_copy(step, head_node.at[my_node], head_node.at[my_node], hn_sems)
        copy.start()
        hns.append(copy)

    total = g_part[me]
    for step, copy in enumerate(grs, 1):
        copy.wait_recv()
        total += g_recv[step].astype(F32)
    g_node[my_node] = total.astype(BF16)
    gns = []
    for step in range(1, nodes):
        copy = node_copy(step, g_node.at[my_node], g_node.at[my_node], gn_sems)
        copy.start()
        gns.append(copy)

    for copy in hns:
        copy.wait_recv()
    total = head_node[0]
    for node in range(1, nodes):
        total += head_node[node]
    head_all[me] = total
    hags = []
    for step in range(1, parts):
        copy = feat_copy(step, head_all.at[me], head_all.at[me], hag_sems)
        copy.start()
        hags.append(copy)

    for copy in gns:
        copy.wait_recv()
    total = g_node[0].astype(F32)
    for node in range(1, nodes):
        total += g_node[node].astype(F32)
    grads_ref[...] = total

    for copy in hags:
        copy.wait_recv()
    head_ref[...] = head_all[...].reshape(head_ref.shape)
    for copy in (*w_copies, *own_copies, *agg_copies, *hrs, *grs, *hns, *gns, *hags):
        copy.wait_send()


def main_call(parts, nodes, counts, near, adj, own, wt, w_head, grad_scores):
    width = near.shape[1]
    targets, out = grad_scores.shape
    hid = w_head.shape[1]
    vmem = pl.BlockSpec(memory_space=pltpu.VMEM)
    smem = pl.BlockSpec(memory_space=pltpu.SMEM)
    head_rows = out // parts
    feat_sems = pltpu.SemaphoreType.DMA((2, parts))
    node_sems = pltpu.SemaphoreType.DMA((2, nodes))
    return pl.pallas_call(
        functools.partial(main_kernel, parts, nodes),
        out_shape=(
            jax.ShapeDtypeStruct((targets, out), BF16),
            jax.ShapeDtypeStruct((2 * width, hid), F32),
            jax.ShapeDtypeStruct((out, hid), F32),
        ),
        in_specs=[smem] + [vmem] * 6,
        out_specs=(vmem, vmem, vmem),
        scratch_shapes=[
            pltpu.VMEM((parts, 2 * width, targets), BF16),
            pltpu.VMEM((parts, 2 * width, hid), BF16),
            pltpu.VMEM((parts, width, targets), BF16),
            pltpu.VMEM((parts, head_rows, hid), F32),
            pltpu.VMEM((parts, head_rows, hid), F32),
            pltpu.VMEM((nodes, head_rows, hid), F32),
            pltpu.VMEM((parts, head_rows, hid), F32),
            pltpu.VMEM((parts, 2 * width, hid), F32),
            pltpu.VMEM((parts, 2 * width, hid), BF16),
            pltpu.VMEM((parts, 2 * width, hid), BF16),
            pltpu.VMEM((nodes, 2 * width, hid), BF16),
            feat_sems, feat_sems, feat_sems, feat_sems, feat_sems, node_sems, node_sems, feat_sems,
        ],
        compiler_params=pltpu.CompilerParams(
            collective_id=0, has_side_effects=True, vmem_limit_bytes=VMEM_BYTES
        ),
        name="train_step",
    )(counts, near, adj, own, wt, w_head, grad_scores)


def solution(mesh):
    parts, nodes = mesh.shape["feat"], mesh.shape["node"]

    def body(
        features, target_ids, block_ids, tile_counts, adjacency, w_neigh, w_self, w_head, grad_scores
    ):
        feat = features[0]
        width = feat.shape[0]
        counts = tile_counts[0]
        own, near, wt = gather_own(
            target_ids[0], block_ids[0].reshape(-1), counts, feat, w_neigh, w_self, parts
        )
        scores, grads, head = main_call(
            parts, nodes, counts.astype(F32), near, adjacency[0], own, wt, w_head, grad_scores[0]
        )
        return scores[None], head, grads[:width].T, grads[width:].T

    in_specs = (
        P("node", "feat", None),
        P("node", None),
        P("node", None, None),
        P("node", None),
        P("node", None, None, None, None),
        P(None, "feat"),
        P(None, "feat"),
        P(),
        P("node", "feat", None),
    )
    out_specs = (P("node", "feat", None), P(), P(None, "feat"), P(None, "feat"))
    return jax.shard_map(body, mesh=mesh, in_specs=in_specs, out_specs=out_specs, check_vma=False)
```

```python
import functools

import jax
import jax.numpy as jnp
from jax import lax
from jax.experimental import pallas as pl
from jax.experimental.pallas import tpu as pltpu
from jax.sharding import PartitionSpec as P

F32 = jnp.float32
BF16 = jnp.bfloat16
VMEM_BYTES = 56 * 1024 * 1024


def nn(left, right):
    return lax.dot_general(left, right, (((1,), (0,)), ((), ())), preferred_element_type=F32)


def nt(left, right):
    return lax.dot_general(left, right, (((1,), (1,)), ((), ())), preferred_element_type=F32)


def gather_kernel(
    ids_ref, blocks_ref, counts_ref, feat_ref, wn_ref, ws_ref, own_ref, near_out, wt_ref, inv_ref,
    table, rows, near_ref, near_sem,
):
    width, sources = feat_ref.shape
    parts, _, targets = own_ref.shape
    wt_ref[:width, :] = wn_ref[...]
    wt_ref[width:, :] = ws_ref[...]

    tiles = near_ref.shape[0]
    slots = near_ref.shape[2] // 128

    def neighbours(tile, carry):
        count = counts_ref[tile]
        inv_ref[pl.ds(tile, 1), :] = 1.0 / jnp.full((1, 128), count.astype(F32), F32)
        for slot in range(slots):
            at = pl.multiple_of(blocks_ref[slot, tile] * 128, 128)
            live = jnp.full((width, 128), (slot < count).astype(F32), F32).astype(BF16)
            near_ref[tile, :, slot * 128 : slot * 128 + 128] = feat_ref[:, pl.ds(at, 128)] * live
        return carry

    lax.fori_loop(0, tiles, neighbours, 0)
    near_copy = pltpu.make_async_copy(near_ref, near_out, near_sem)
    near_copy.start()

    def fill(step, carry):
        for piece in range(4):
            at = pl.multiple_of((step * 4 + piece) * 128, 128)
            table[pl.ds(at, 128), :] = feat_ref[:, pl.ds(at, 128)].astype(F32).T
        return carry

    lax.fori_loop(0, sources // 512, fill, 0)

    def chunk(step, carry):
        base = step * 128
        for row in range(128):
            rows[row : row + 1, :] = table[pl.ds(ids_ref[base + row], 1), :]
        part = base // targets
        inside = pl.multiple_of(base - part * targets, 128)
        own_ref[part, :, pl.ds(inside, 128)] = rows[...].T.astype(BF16)
        return carry

    lax.fori_loop(0, parts * targets // 128, chunk, 0)
    near_copy.wait()


def gather_own(ids, blocks, counts, feat, w_neigh, w_self, parts):
    width, sources = feat.shape
    hid = w_neigh.shape[1]
    targets = ids.shape[0] // parts
    slots, tiles = blocks.shape
    vmem = pl.BlockSpec(memory_space=pltpu.VMEM)
    smem = pl.BlockSpec(memory_space=pltpu.SMEM)
    return pl.pallas_call(
        gather_kernel,
        out_shape=(
            jax.ShapeDtypeStruct((parts, width, targets), BF16),
            jax.ShapeDtypeStruct((tiles, width, slots * 128), BF16),
            jax.ShapeDtypeStruct((2 * width, hid), BF16),
            jax.ShapeDtypeStruct((tiles, 128), F32),
        ),
        in_specs=[smem, smem, smem, vmem, vmem, vmem],
        out_specs=(vmem, pl.BlockSpec(memory_space=pl.ANY), vmem, vmem),
        scratch_shapes=[
            pltpu.VMEM((sources, width), F32),
            pltpu.VMEM((128, width), F32),
            pltpu.VMEM((tiles, width, slots * 128), BF16),
            pltpu.SemaphoreType.DMA,
        ],
        compiler_params=pltpu.CompilerParams(vmem_limit_bytes=VMEM_BYTES),
        name="own_gather",
    )(ids, blocks, counts, feat, w_neigh, w_self)


def main_kernel(
    parts, nodes, inv_ref, near_hbm, adj_hbm, own_ref, wt_ref, wh_ref, gs_ref,
    scores_ref, grads_ref, head_ref,
    near_ref, adj_ref, x_all, w_all, agg_send, head_part, head_recv, head_node, head_all,
    g_part, g_send, g_recv, g_node,
    w_sems, own_sems, agg_sems, hrs_sems, grs_sems, hn_sems, gn_sems, hag_sems,
    load_sems,
):
    me = lax.axis_index("feat")
    my_node = lax.axis_index("node")
    width = near_ref.shape[1]
    tiles, slots = adj_ref.shape[:2]
    per_part = tiles // parts
    hid = wh_ref.shape[1]
    targets = gs_ref.shape[0]

    def feat_copy(step, src, dst, sems):
        peer = lax.rem(me + step, parts)
        return pltpu.make_async_remote_copy(
            src_ref=src, dst_ref=dst, send_sem=sems.at[0, step], recv_sem=sems.at[1, step],
            device_id={"feat": peer}, device_id_type=pl.DeviceIdType.MESH,
        )

    def node_copy(step, src, dst, sems):
        peer = lax.rem(my_node + step, nodes)
        return pltpu.make_async_remote_copy(
            src_ref=src, dst_ref=dst, send_sem=sems.at[0, step], recv_sem=sems.at[1, step],
            device_id={"node": peer}, device_id_type=pl.DeviceIdType.MESH,
        )

    loads = []
    for step in range(1, parts + 1):
        first = lax.rem(me + step, parts) * per_part
        for which, (src, dst) in enumerate(((near_hbm, near_ref), (adj_hbm, adj_ref))):
            copy = pltpu.make_async_copy(
                src.at[pl.ds(first, per_part)],
                dst.at[pl.ds((step - 1) * per_part, per_part)],
                load_sems.at[which, step - 1],
            )
            copy.start()
            loads.append(copy)

    barrier = pltpu.get_barrier_semaphore()
    for step in range(1, parts):
        pl.semaphore_signal(
            barrier, inc=1, device_id={"feat": lax.rem(me + step, parts)},
            device_id_type=pl.DeviceIdType.MESH,
        )
    for step in range(1, nodes):
        pl.semaphore_signal(
            barrier, inc=1, device_id={"node": lax.rem(my_node + step, nodes)},
            device_id_type=pl.DeviceIdType.MESH,
        )
    pl.semaphore_wait(barrier, parts + nodes - 2)

    w_copies, own_copies, agg_copies = [], [], []
    for step in range(1, parts):
        peer = lax.rem(me + step, parts)
        copy = feat_copy(step, own_ref.at[peer], x_all.at[me, pl.ds(width, width)], own_sems)
        copy.start()
        own_copies.append(copy)
        copy = feat_copy(step, wt_ref, w_all.at[me], w_sems)
        copy.start()
        w_copies.append(copy)

    def aggregate(held, tile):
        edges = jnp.concatenate([adj_ref[held, slot] for slot in range(slots)], axis=1)
        return (nt(near_ref[held], edges) * inv_ref[pl.ds(tile, 1), :]).astype(BF16)

    for step in range(1, parts + 1):
        peer = lax.rem(me + step, parts)
        loads[2 * step - 2].wait()
        loads[2 * step - 1].wait()
        for tile in range(per_part):
            part = aggregate((step - 1) * per_part + tile, peer * per_part + tile)
            if step < parts:
                agg_send[step, :, tile * 128 : tile * 128 + 128] = part
            else:
                x_all[me, :width, tile * 128 : tile * 128 + 128] = part
        if step < parts:
            copy = feat_copy(step, agg_send.at[step], x_all.at[me, pl.ds(0, width)], agg_sems)
            copy.start()
            agg_copies.append(copy)
    x_all[me, width:, :] = own_ref[me]
    w_all[me] = wt_ref[...]

    grad_t = gs_ref[...].astype(F32).T.astype(BF16)
    head_t = wh_ref[...].astype(F32).T.astype(BF16)
    grad_hidden = nn(head_t, grad_t)

    for copy in w_copies:
        copy.wait_recv()
    weights = w_all[...].reshape(parts * 2 * width, hid).astype(F32).T.astype(BF16)
    for copy in own_copies:
        copy.wait_recv()
    for copy in agg_copies:
        copy.wait_recv()
    x = x_all[...].reshape(parts * 2 * width, targets)
    preact = nn(weights, x)
    sigma = 1.0 / (1.0 + jnp.exp(-preact))
    hidden = (preact * sigma).astype(BF16)
    head_part[...] = nt(grad_t, hidden).reshape(head_part.shape)
    hrs = []
    for step in range(1, parts):
        peer = lax.rem(me + step, parts)
        copy = feat_copy(step, head_part.at[peer], head_recv.at[step], hrs_sems)
        copy.start()
        hrs.append(copy)
    grad_pre = (grad_hidden * sigma * (1.0 + preact * (1.0 - sigma))).astype(BF16)
    grads = nt(x, grad_pre).reshape(g_part.shape)
    g_part[...] = grads
    g_send[...] = grads.astype(BF16)
    grs = []
    for step in range(1, parts):
        peer = lax.rem(me + step, parts)
        copy = feat_copy(step, g_send.at[peer], g_recv.at[step], grs_sems)
        copy.start()
        grs.append(copy)
    scores_ref[...] = nn(wh_ref[...], hidden).T.astype(BF16)

    total = head_part[me]
    for step, copy in enumerate(hrs, 1):
        copy.wait_recv()
        total += head_recv[step]
    head_node[my_node] = total
    hns = []
    for step in range(1, nodes):
        copy = node_copy(step, head_node.at[my_node], head_node.at[my_node], hn_sems)
        copy.start()
        hns.append(copy)

    total = g_part[me]
    for step, copy in enumerate(grs, 1):
        copy.wait_recv()
        total += g_recv[step].astype(F32)
    g_node[my_node] = total.astype(BF16)
    gns = []
    for step in range(1, nodes):
        copy = node_copy(step, g_node.at[my_node], g_node.at[my_node], gn_sems)
        copy.start()
        gns.append(copy)

    for copy in hns:
        copy.wait_recv()
    total = head_node[0]
    for node in range(1, nodes):
        total += head_node[node]
    head_all[me] = total
    hags = []
    for step in range(1, parts):
        copy = feat_copy(step, head_all.at[me], head_all.at[me], hag_sems)
        copy.start()
        hags.append(copy)

    for copy in gns:
        copy.wait_recv()
    total = g_node[0].astype(F32)
    for node in range(1, nodes):
        total += g_node[node].astype(F32)
    grads_ref[...] = total

    for copy in hags:
        copy.wait_recv()
    head_ref[...] = head_all[...].reshape(head_ref.shape)
    for copy in (*w_copies, *own_copies, *agg_copies, *hrs, *grs, *hns, *gns, *hags):
        copy.wait_send()


def main_call(parts, nodes, inv, near, adj, own, wt, w_head, grad_scores):
    width = near.shape[1]
    targets, out = grad_scores.shape
    hid = w_head.shape[1]
    vmem = pl.BlockSpec(memory_space=pltpu.VMEM)
    anywhere = pl.BlockSpec(memory_space=pl.ANY)
    head_rows = out // parts
    feat_sems = pltpu.SemaphoreType.DMA((2, parts))
    node_sems = pltpu.SemaphoreType.DMA((2, nodes))
    return pl.pallas_call(
        functools.partial(main_kernel, parts, nodes),
        out_shape=(
            jax.ShapeDtypeStruct((targets, out), BF16),
            jax.ShapeDtypeStruct((2 * width, hid), F32),
            jax.ShapeDtypeStruct((out, hid), F32),
        ),
        in_specs=[vmem, anywhere, anywhere] + [vmem] * 4,
        out_specs=(vmem, vmem, vmem),
        scratch_shapes=[
            pltpu.VMEM(near.shape, BF16),
            pltpu.VMEM(adj.shape, BF16),
            pltpu.VMEM((parts, 2 * width, targets), BF16),
            pltpu.VMEM((parts, 2 * width, hid), BF16),
            pltpu.VMEM((parts, width, targets), BF16),
            pltpu.VMEM((parts, head_rows, hid), F32),
            pltpu.VMEM((parts, head_rows, hid), F32),
            pltpu.VMEM((nodes, head_rows, hid), F32),
            pltpu.VMEM((parts, head_rows, hid), F32),
            pltpu.VMEM((parts, 2 * width, hid), F32),
            pltpu.VMEM((parts, 2 * width, hid), BF16),
            pltpu.VMEM((parts, 2 * width, hid), BF16),
            pltpu.VMEM((nodes, 2 * width, hid), BF16),
            feat_sems, feat_sems, feat_sems, feat_sems, feat_sems, node_sems, node_sems, feat_sems,
            pltpu.SemaphoreType.DMA((2, parts)),
        ],
        compiler_params=pltpu.CompilerParams(
            collective_id=0, has_side_effects=True, vmem_limit_bytes=VMEM_BYTES
        ),
        name="train_step",
    )(inv, near, adj, own, wt, w_head, grad_scores)


def hand_over_kernel(scores_in, head_in, grads_in, scores_ref, head_ref, neigh_ref, self_ref):
    width = neigh_ref.shape[0]
    scores_ref[...] = scores_in[...]
    head_ref[...] = head_in[...]
    neigh_ref[...] = grads_in[:width, :]
    self_ref[...] = grads_in[width:, :]


def hand_over(scores, head, grads):
    vmem = pl.BlockSpec(memory_space=pltpu.VMEM)
    half = jax.ShapeDtypeStruct((grads.shape[0] // 2, grads.shape[1]), F32)
    return pl.pallas_call(
        hand_over_kernel,
        out_shape=(
            jax.ShapeDtypeStruct(scores.shape, BF16), jax.ShapeDtypeStruct(head.shape, F32), half, half,
        ),
        in_specs=[vmem] * 3,
        out_specs=(vmem,) * 4,
        name="hand_over",
    )(scores, head, grads)


def solution(mesh):
    parts, nodes = mesh.shape["feat"], mesh.shape["node"]

    def body(
        features, target_ids, block_ids, tile_counts, adjacency, w_neigh, w_self, w_head, grad_scores
    ):
        feat = features[0]
        counts = tile_counts[0]
        own, near, wt, inv = gather_own(
            target_ids[0], block_ids[0].T, counts, feat, w_neigh.T, w_self.T, parts
        )
        scores, grads, head = main_call(
            parts, nodes, inv, near, adjacency[0], own, wt, w_head, grad_scores[0]
        )
        scores, head, neigh, own_grad = hand_over(scores, head, grads)
        return scores[None], head, neigh.T, own_grad.T

    in_specs = (
        P("node", "feat", None),
        P("node", None),
        P("node", None, None),
        P("node", None),
        P("node", None, None, None, None),
        P(None, "feat"),
        P(None, "feat"),
        P(),
        P("node", "feat", None),
    )
    out_specs = (P("node", "feat", None), P(), P(None, "feat"), P(None, "feat"))
    return jax.shard_map(body, mesh=mesh, in_specs=in_specs, out_specs=out_specs, check_vma=False)
```

```python
import functools

import jax
import jax.numpy as jnp
from jax import lax
from jax.experimental import pallas as pl
from jax.experimental.pallas import tpu as pltpu
from jax.sharding import PartitionSpec as P

F32 = jnp.float32
BF16 = jnp.bfloat16
VMEM_BYTES = 56 * 1024 * 1024


def nn(left, right):
    return lax.dot_general(left, right, (((1,), (0,)), ((), ())), preferred_element_type=F32)


def nt(left, right):
    return lax.dot_general(left, right, (((1,), (1,)), ((), ())), preferred_element_type=F32)


def gather_kernel(
    ids_ref, blocks_ref, counts_ref, feat_ref, own_ref, near_out, inv_ref,
    table, rows, near_ref, near_sem,
):
    width, sources = feat_ref.shape
    parts, _, targets = own_ref.shape
    tiles = near_ref.shape[0]
    slots = near_ref.shape[2] // 128

    def neighbours(tile, carry):
        count = counts_ref[tile]
        inv_ref[pl.ds(tile, 1), :] = 1.0 / jnp.full((1, 128), count.astype(F32), F32)
        for slot in range(slots):
            at = pl.multiple_of(blocks_ref[slot, tile] * 128, 128)
            live = jnp.full((width, 128), (slot < count).astype(F32), F32).astype(BF16)
            near_ref[tile, :, slot * 128 : slot * 128 + 128] = feat_ref[:, pl.ds(at, 128)] * live
        return carry

    lax.fori_loop(0, tiles, neighbours, 0)
    near_copy = pltpu.make_async_copy(near_ref, near_out, near_sem)
    near_copy.start()

    def fill(step, carry):
        for piece in range(4):
            at = pl.multiple_of((step * 4 + piece) * 128, 128)
            table[pl.ds(at, 128), :] = feat_ref[:, pl.ds(at, 128)].astype(F32).T
        return carry

    lax.fori_loop(0, sources // 512, fill, 0)

    def chunk(step, carry):
        base = step * 128
        for row in range(128):
            rows[row : row + 1, :] = table[pl.ds(ids_ref[base + row], 1), :]
        part = base // targets
        inside = pl.multiple_of(base - part * targets, 128)
        own_ref[part, :, pl.ds(inside, 128)] = rows[...].T.astype(BF16)
        return carry

    lax.fori_loop(0, parts * targets // 128, chunk, 0)
    near_copy.wait()


def gather_own(ids, blocks, counts, feat, parts):
    width, sources = feat.shape
    targets = ids.shape[0] // parts
    slots, tiles = blocks.shape
    vmem = pl.BlockSpec(memory_space=pltpu.VMEM)
    smem = pl.BlockSpec(memory_space=pltpu.SMEM)
    return pl.pallas_call(
        gather_kernel,
        out_shape=(
            jax.ShapeDtypeStruct((parts, width, targets), BF16),
            jax.ShapeDtypeStruct((tiles, width, slots * 128), BF16),
            jax.ShapeDtypeStruct((tiles, 128), F32),
        ),
        in_specs=[smem, smem, smem, vmem],
        out_specs=(vmem, pl.BlockSpec(memory_space=pl.ANY), vmem),
        scratch_shapes=[
            pltpu.VMEM((sources, width), F32),
            pltpu.VMEM((128, width), F32),
            pltpu.VMEM((tiles, width, slots * 128), BF16),
            pltpu.SemaphoreType.DMA,
        ],
        compiler_params=pltpu.CompilerParams(vmem_limit_bytes=VMEM_BYTES),
        cost_estimate=pl.CostEstimate(flops=0, bytes_accessed=48 << 20, transcendentals=0),
        name="own_gather",
    )(ids, blocks, counts, feat)


def main_kernel(
    parts, nodes, inv_ref, near_hbm, adj_hbm, own_ref, wn_ref, ws_ref, wh_ref, gs_ref,
    scores_ref, grads_ref, head_ref,
    near_ref, adj_ref, x_all, agg_send, head_part, head_sib, head_send, head_recv, head_node, head_all,
    g_part, g_sib, g_send, g_recv, g_node,
    pair_sems, own_sems, agg_sems, hrs_sems, grs_sems, hn_sems, gn_sems, hag_sems,
    load_sems,
):
    me = lax.axis_index("feat")
    my_node = lax.axis_index("node")
    width = near_ref.shape[1]
    tiles, slots = adj_ref.shape[:2]
    per_part = tiles // parts
    hid = wh_ref.shape[1]
    targets = gs_ref.shape[0]

    def feat_copy(step, src, dst, sems):
        peer = lax.rem(me + step, parts)
        return pltpu.make_async_remote_copy(
            src_ref=src, dst_ref=dst, send_sem=sems.at[0, step], recv_sem=sems.at[1, step],
            device_id={"feat": peer}, device_id_type=pl.DeviceIdType.MESH,
        )

    chips = parts // 2
    chip, core = me // 2, lax.rem(me, 2)
    mate = 1 - core

    def chip_copy(step, src, dst, sems):
        return pltpu.make_async_remote_copy(
            src_ref=src, dst_ref=dst, send_sem=sems.at[0, step], recv_sem=sems.at[1, step],
            device_id={"feat": lax.rem(chip + step, chips) * 2 + core},
            device_id_type=pl.DeviceIdType.MESH,
        )

    def pair_copy(which, src, dst):
        return pltpu.make_async_remote_copy(
            src_ref=src, dst_ref=dst, send_sem=pair_sems.at[0, which], recv_sem=pair_sems.at[1, which],
            device_id={"feat": chip * 2 + mate}, device_id_type=pl.DeviceIdType.MESH,
        )

    def node_copy(step, src, dst, sems):
        peer = lax.rem(my_node + step, nodes)
        return pltpu.make_async_remote_copy(
            src_ref=src, dst_ref=dst, send_sem=sems.at[0, step], recv_sem=sems.at[1, step],
            device_id={"node": peer}, device_id_type=pl.DeviceIdType.MESH,
        )

    loads = []
    for step in range(1, parts + 1):
        first = lax.rem(me + step, parts) * per_part
        for which, (src, dst) in enumerate(((near_hbm, near_ref), (adj_hbm, adj_ref))):
            copy = pltpu.make_async_copy(
                src.at[pl.ds(first, per_part)],
                dst.at[pl.ds((step - 1) * per_part, per_part)],
                load_sems.at[which, step - 1],
            )
            copy.start()
            loads.append(copy)

    barrier = pltpu.get_barrier_semaphore()
    for step in range(1, parts):
        pl.semaphore_signal(
            barrier, inc=1, device_id={"feat": lax.rem(me + step, parts)},
            device_id_type=pl.DeviceIdType.MESH,
        )
    for step in range(1, nodes):
        pl.semaphore_signal(
            barrier, inc=1, device_id={"node": lax.rem(my_node + step, nodes)},
            device_id_type=pl.DeviceIdType.MESH,
        )
    pl.semaphore_wait(barrier, parts + nodes - 2)

    own_copies, agg_copies = [], []
    for step in range(1, parts):
        peer = lax.rem(me + step, parts)
        copy = feat_copy(step, own_ref.at[peer], x_all.at[me, pl.ds(width, width)], own_sems)
        copy.start()
        own_copies.append(copy)

    def aggregate(held, tile):
        edges = jnp.concatenate([adj_ref[held, slot] for slot in range(slots)], axis=1)
        return (nt(near_ref[held], edges) * inv_ref[pl.ds(tile, 1), :]).astype(BF16)

    for step in range(1, parts + 1):
        peer = lax.rem(me + step, parts)
        loads[2 * step - 2].wait()
        loads[2 * step - 1].wait()
        for tile in range(per_part):
            part = aggregate((step - 1) * per_part + tile, peer * per_part + tile)
            if step < parts:
                agg_send[step, :, tile * 128 : tile * 128 + 128] = part
            else:
                x_all[me, :width, tile * 128 : tile * 128 + 128] = part
        if step < parts:
            copy = feat_copy(step, agg_send.at[step], x_all.at[me, pl.ds(0, width)], agg_sems)
            copy.start()
            agg_copies.append(copy)
    x_all[me, width:, :] = own_ref[me]

    grad_t = gs_ref[...].astype(F32).T.astype(BF16)
    head_t = wh_ref[...].astype(F32).T.astype(BF16)
    grad_hidden = nn(head_t, grad_t)

    weights = jnp.concatenate(
        [
            wn_ref[...].reshape(parts, width, hid).astype(F32),
            ws_ref[...].reshape(parts, width, hid).astype(F32),
        ],
        axis=1,
    )
    weights = weights.reshape(parts * 2 * width, hid).T.astype(BF16)
    for copy in own_copies:
        copy.wait_recv()
    for copy in agg_copies:
        copy.wait_recv()
    x = x_all[...].reshape(parts * 2 * width, targets)
    preact = nn(weights, x)
    sigma = 1.0 / (1.0 + jnp.exp(-preact))
    hidden = (preact * sigma).astype(BF16)
    head_part[...] = nt(grad_t, hidden).reshape(head_part.shape)
    head_pair = pair_copy(0, head_part.at[:, mate], head_sib)
    head_pair.start()
    grad_pre = (grad_hidden * sigma * (1.0 + preact * (1.0 - sigma))).astype(BF16)
    grads = nt(x, grad_pre).reshape(g_part.shape)
    g_part[...] = grads
    g_pair = pair_copy(1, g_part.at[:, mate], g_sib)
    g_pair.start()

    head_pair.wait_recv()
    hrs = []
    for step in range(1, chips):
        to = lax.rem(chip + step, chips)
        head_send[step] = head_part[to, core] + head_sib[to]
        copy = chip_copy(step, head_send.at[step], head_recv.at[step], hrs_sems)
        copy.start()
        hrs.append(copy)
    g_pair.wait_recv()
    grs = []
    for step in range(1, chips):
        to = lax.rem(chip + step, chips)
        g_send[step] = (g_part[to, core] + g_sib[to]).astype(BF16)
        copy = chip_copy(step, g_send.at[step], g_recv.at[step], grs_sems)
        copy.start()
        grs.append(copy)
    scores_ref[...] = nn(wh_ref[...], hidden).T.astype(BF16)

    total = head_part[chip, core] + head_sib[chip]
    for step, copy in enumerate(hrs, 1):
        copy.wait_recv()
        total += head_recv[step]
    head_node[my_node] = total
    hns = []
    for step in range(1, nodes):
        copy = node_copy(step, head_node.at[my_node], head_node.at[my_node], hn_sems)
        copy.start()
        hns.append(copy)

    total = g_part[chip, core] + g_sib[chip]
    for step, copy in enumerate(grs, 1):
        copy.wait_recv()
        total += g_recv[step].astype(F32)
    g_node[my_node] = total.astype(BF16)
    gns = []
    for step in range(1, nodes):
        copy = node_copy(step, g_node.at[my_node], g_node.at[my_node], gn_sems)
        copy.start()
        gns.append(copy)

    for copy in hns:
        copy.wait_recv()
    total = head_node[0]
    for node in range(1, nodes):
        total += head_node[node]
    head_all[me] = total
    hags = []
    for step in range(1, parts):
        copy = feat_copy(step, head_all.at[me], head_all.at[me], hag_sems)
        copy.start()
        hags.append(copy)

    for copy in gns:
        copy.wait_recv()
    total = g_node[0].astype(F32)
    for node in range(1, nodes):
        total += g_node[node].astype(F32)
    grads_ref[...] = total

    for copy in hags:
        copy.wait_recv()
    head_ref[...] = head_all[...].reshape(head_ref.shape)
    for copy in (head_pair, g_pair, *own_copies, *agg_copies, *hrs, *grs, *hns, *gns, *hags):
        copy.wait_send()


def main_call(parts, nodes, inv, near, adj, own, wn, ws, w_head, grad_scores):
    width = near.shape[1]
    targets, out = grad_scores.shape
    hid = w_head.shape[1]
    vmem = pl.BlockSpec(memory_space=pltpu.VMEM)
    anywhere = pl.BlockSpec(memory_space=pl.ANY)
    head_rows = out // parts
    feat_sems = pltpu.SemaphoreType.DMA((2, parts))
    chips = parts // 2
    chip_sems = pltpu.SemaphoreType.DMA((2, chips))
    node_sems = pltpu.SemaphoreType.DMA((2, nodes))
    return pl.pallas_call(
        functools.partial(main_kernel, parts, nodes),
        out_shape=(
            jax.ShapeDtypeStruct((targets, out), BF16),
            jax.ShapeDtypeStruct((2 * width, hid), F32),
            jax.ShapeDtypeStruct((out, hid), F32),
        ),
        in_specs=[vmem, anywhere, anywhere] + [vmem] * 5,
        out_specs=(vmem, vmem, vmem),
        scratch_shapes=[
            pltpu.VMEM(near.shape, BF16),
            pltpu.VMEM(adj.shape, BF16),
            pltpu.VMEM((parts, 2 * width, targets), BF16),
            pltpu.VMEM((parts, width, targets), BF16),
            pltpu.VMEM((chips, 2, head_rows, hid), F32),
            pltpu.VMEM((chips, head_rows, hid), F32),
            pltpu.VMEM((chips, head_rows, hid), F32),
            pltpu.VMEM((chips, head_rows, hid), F32),
            pltpu.VMEM((nodes, head_rows, hid), F32),
            pltpu.VMEM((parts, head_rows, hid), F32),
            pltpu.VMEM((chips, 2, 2 * width, hid), F32),
            pltpu.VMEM((chips, 2 * width, hid), F32),
            pltpu.VMEM((chips, 2 * width, hid), BF16),
            pltpu.VMEM((chips, 2 * width, hid), BF16),
            pltpu.VMEM((nodes, 2 * width, hid), BF16),
            pltpu.SemaphoreType.DMA((2, 2)), feat_sems, feat_sems, chip_sems, chip_sems, node_sems, node_sems, feat_sems,
            pltpu.SemaphoreType.DMA((2, parts)),
        ],
        compiler_params=pltpu.CompilerParams(
            collective_id=0, has_side_effects=True, vmem_limit_bytes=VMEM_BYTES
        ),
        name="train_step",
    )(inv, near, adj, own, wn, ws, w_head, grad_scores)


def hand_over_kernel(scores_in, head_in, grads_in, scores_ref, head_ref, neigh_ref, self_ref):
    width = neigh_ref.shape[0]
    scores_ref[...] = scores_in[...]
    head_ref[...] = head_in[...]
    neigh_ref[...] = grads_in[:width, :]
    self_ref[...] = grads_in[width:, :]


def hand_over(scores, head, grads):
    vmem = pl.BlockSpec(memory_space=pltpu.VMEM)
    half = jax.ShapeDtypeStruct((grads.shape[0] // 2, grads.shape[1]), F32)
    return pl.pallas_call(
        hand_over_kernel,
        out_shape=(
            jax.ShapeDtypeStruct(scores.shape, BF16), jax.ShapeDtypeStruct(head.shape, F32), half, half,
        ),
        in_specs=[vmem] * 3,
        out_specs=(vmem,) * 4,
        name="hand_over",
    )(scores, head, grads)


def solution(mesh):
    parts, nodes = mesh.shape["feat"], mesh.shape["node"]

    def body(
        features, target_ids, block_ids, tile_counts, adjacency, w_neigh, w_self, w_head, grad_scores
    ):
        feat = features[0]
        counts = tile_counts[0]
        wn = lax.all_gather(w_neigh.T, "feat", axis=0, tiled=True)
        ws = lax.all_gather(w_self.T, "feat", axis=0, tiled=True)
        own, near, inv = gather_own(target_ids[0], block_ids[0].T, counts, feat, parts)
        scores, grads, head = main_call(
            parts, nodes, inv, near, adjacency[0], own, wn, ws, w_head, grad_scores[0]
        )
        scores, head, neigh, own_grad = hand_over(scores, head, grads)
        return scores[None], head, neigh.T, own_grad.T

    in_specs = (
        P("node", "feat", None),
        P("node", None),
        P("node", None, None),
        P("node", None),
        P("node", None, None, None, None),
        P(None, "feat"),
        P(None, "feat"),
        P(),
        P("node", "feat", None),
    )
    out_specs = (P("node", "feat", None), P(), P(None, "feat"), P(None, "feat"))
    return jax.shard_map(body, mesh=mesh, in_specs=in_specs, out_specs=out_specs, check_vma=False)
```

```python
import functools

import jax
import jax.numpy as jnp
from jax import lax
from jax.experimental import pallas as pl
from jax.experimental.pallas import tpu as pltpu
from jax.sharding import PartitionSpec as P

F32 = jnp.float32
BF16 = jnp.bfloat16
VMEM_BYTES = 56 * 1024 * 1024


def nn(left, right):
    return lax.dot_general(left, right, (((1,), (0,)), ((), ())), preferred_element_type=F32)


def nt(left, right):
    return lax.dot_general(left, right, (((1,), (1,)), ((), ())), preferred_element_type=F32)


def gather_kernel(
    ids_ref, blocks_ref, counts_ref, feat_ref, wn_ref, ws_ref, own_ref, near_out, wt_ref, inv_ref,
    table, rows, near_ref, near_sem,
):
    width, sources = feat_ref.shape
    parts, _, targets = own_ref.shape
    wt_ref[:width, :] = wn_ref[...]
    wt_ref[width:, :] = ws_ref[...]
    tiles = near_ref.shape[0]
    slots = near_ref.shape[2] // 128

    def neighbours(tile, carry):
        count = counts_ref[tile]
        inv_ref[pl.ds(tile, 1), :] = 1.0 / jnp.full((1, 128), count.astype(F32), F32)
        for slot in range(slots):
            at = pl.multiple_of(blocks_ref[slot, tile] * 128, 128)
            live = jnp.full((width, 128), (slot < count).astype(F32), F32).astype(BF16)
            near_ref[tile, :, slot * 128 : slot * 128 + 128] = feat_ref[:, pl.ds(at, 128)] * live
        return carry

    lax.fori_loop(0, tiles, neighbours, 0)
    near_copy = pltpu.make_async_copy(near_ref, near_out, near_sem)
    near_copy.start()

    def fill(step, carry):
        for piece in range(4):
            at = pl.multiple_of((step * 4 + piece) * 128, 128)
            table[pl.ds(at, 128), :] = feat_ref[:, pl.ds(at, 128)].astype(F32).T
        return carry

    lax.fori_loop(0, sources // 512, fill, 0)

    def chunk(step, carry):
        base = step * 128
        for row in range(128):
            rows[row : row + 1, :] = table[pl.ds(ids_ref[base + row], 1), :]
        part = base // targets
        inside = pl.multiple_of(base - part * targets, 128)
        own_ref[part, :, pl.ds(inside, 128)] = rows[...].T.astype(BF16)
        return carry

    lax.fori_loop(0, parts * targets // 128, chunk, 0)
    near_copy.wait()


def gather_own(ids, blocks, counts, feat, w_neigh, w_self, parts):
    width, sources = feat.shape
    targets = ids.shape[0] // parts
    slots, tiles = blocks.shape
    vmem = pl.BlockSpec(memory_space=pltpu.VMEM)
    smem = pl.BlockSpec(memory_space=pltpu.SMEM)
    return pl.pallas_call(
        gather_kernel,
        out_shape=(
            jax.ShapeDtypeStruct((parts, width, targets), BF16),
            jax.ShapeDtypeStruct((tiles, width, slots * 128), BF16),
            jax.ShapeDtypeStruct((2 * width, w_neigh.shape[1]), BF16),
            jax.ShapeDtypeStruct((tiles, 128), F32),
        ),
        in_specs=[smem, smem, smem, vmem, vmem, vmem],
        out_specs=(vmem, pl.BlockSpec(memory_space=pl.ANY), vmem, vmem),
        scratch_shapes=[
            pltpu.VMEM((sources, width), F32),
            pltpu.VMEM((128, width), F32),
            pltpu.VMEM((tiles, width, slots * 128), BF16),
            pltpu.SemaphoreType.DMA,
        ],
        compiler_params=pltpu.CompilerParams(vmem_limit_bytes=VMEM_BYTES),
        cost_estimate=pl.CostEstimate(flops=0, bytes_accessed=48 << 20, transcendentals=0),
        name="own_gather",
    )(ids, blocks, counts, feat, w_neigh, w_self)


def main_kernel(
    parts, nodes, inv_ref, near_hbm, adj_hbm, own_ref, wt_ref, wh_ref, gs_ref,
    scores_ref, grads_ref, head_ref,
    near_ref, adj_ref, x_all, w_all, agg_send, head_part, head_sib, head_send, head_recv, head_node, head_all,
    g_part, g_sib, g_send, g_recv, g_node,
    w_sems, mate_sems, pair_sems, own_sems, agg_sems, hrs_sems, grs_sems, hn_sems, gn_sems, hag_sems,
    load_sems,
):
    me = lax.axis_index("feat")
    my_node = lax.axis_index("node")
    width = near_ref.shape[1]
    tiles, slots = adj_ref.shape[:2]
    per_part = tiles // parts
    hid = wh_ref.shape[1]
    targets = gs_ref.shape[0]

    def feat_copy(step, src, dst, sems):
        peer = lax.rem(me + step, parts)
        return pltpu.make_async_remote_copy(
            src_ref=src, dst_ref=dst, send_sem=sems.at[0, step], recv_sem=sems.at[1, step],
            device_id={"feat": peer}, device_id_type=pl.DeviceIdType.MESH,
        )

    chips = parts // 2
    chip, core = me // 2, lax.rem(me, 2)
    mate = 1 - core

    def chip_copy(step, src, dst, sems):
        return pltpu.make_async_remote_copy(
            src_ref=src, dst_ref=dst, send_sem=sems.at[0, step], recv_sem=sems.at[1, step],
            device_id={"feat": lax.rem(chip + step, chips) * 2 + core},
            device_id_type=pl.DeviceIdType.MESH,
        )

    def pair_copy(which, src, dst):
        return pltpu.make_async_remote_copy(
            src_ref=src, dst_ref=dst, send_sem=pair_sems.at[0, which], recv_sem=pair_sems.at[1, which],
            device_id={"feat": chip * 2 + mate}, device_id_type=pl.DeviceIdType.MESH,
        )

    def node_copy(step, src, dst, sems):
        peer = lax.rem(my_node + step, nodes)
        return pltpu.make_async_remote_copy(
            src_ref=src, dst_ref=dst, send_sem=sems.at[0, step], recv_sem=sems.at[1, step],
            device_id={"node": peer}, device_id_type=pl.DeviceIdType.MESH,
        )

    loads = []
    for step in range(1, parts + 1):
        first = lax.rem(me + step, parts) * per_part
        for which, (src, dst) in enumerate(((near_hbm, near_ref), (adj_hbm, adj_ref))):
            copy = pltpu.make_async_copy(
                src.at[pl.ds(first, per_part)],
                dst.at[pl.ds((step - 1) * per_part, per_part)],
                load_sems.at[which, step - 1],
            )
            copy.start()
            loads.append(copy)

    barrier = pltpu.get_barrier_semaphore()
    for step in range(1, parts):
        pl.semaphore_signal(
            barrier, inc=1, device_id={"feat": lax.rem(me + step, parts)},
            device_id_type=pl.DeviceIdType.MESH,
        )
    for step in range(1, nodes):
        pl.semaphore_signal(
            barrier, inc=1, device_id={"node": lax.rem(my_node + step, nodes)},
            device_id_type=pl.DeviceIdType.MESH,
        )
    pl.semaphore_wait(barrier, parts + nodes - 2)

    w_copies = [
        chip_copy(step, wt_ref, w_all.at[chip, core], w_sems) for step in range(1, chips)
    ]
    for copy in w_copies:
        copy.start()

    def mate_copy(step, src, dst):
        return pltpu.make_async_remote_copy(
            src_ref=src, dst_ref=dst, send_sem=mate_sems.at[0, step], recv_sem=mate_sems.at[1, step],
            device_id={"feat": chip * 2 + mate}, device_id_type=pl.DeviceIdType.MESH,
        )

    mates = [mate_copy(0, wt_ref, w_all.at[chip, core])]
    mates[0].start()
    own_copies, agg_copies = [], []
    for step in range(1, parts):
        peer = lax.rem(me + step, parts)
        copy = feat_copy(step, own_ref.at[peer], x_all.at[me, pl.ds(width, width)], own_sems)
        copy.start()
        own_copies.append(copy)

    def aggregate(held, tile):
        edges = jnp.concatenate([adj_ref[held, slot] for slot in range(slots)], axis=1)
        return (nt(near_ref[held], edges) * inv_ref[pl.ds(tile, 1), :]).astype(BF16)

    for step in range(1, parts + 1):
        peer = lax.rem(me + step, parts)
        loads[2 * step - 2].wait()
        loads[2 * step - 1].wait()
        for tile in range(per_part):
            part = aggregate((step - 1) * per_part + tile, peer * per_part + tile)
            if step < parts:
                agg_send[step, :, tile * 128 : tile * 128 + 128] = part
            else:
                x_all[me, :width, tile * 128 : tile * 128 + 128] = part
        if step < parts:
            copy = feat_copy(step, agg_send.at[step], x_all.at[me, pl.ds(0, width)], agg_sems)
            copy.start()
            agg_copies.append(copy)
    for step, copy in enumerate(w_copies, 1):
        copy.wait_recv()
        held = w_all.at[lax.rem(chip + chips - step, chips), core]
        copy = mate_copy(step, held, held)
        copy.start()
        mates.append(copy)
    w_all[chip, core] = wt_ref[...]
    x_all[me, width:, :] = own_ref[me]

    grad_t = gs_ref[...].astype(F32).T.astype(BF16)
    head_t = wh_ref[...].astype(F32).T.astype(BF16)
    grad_hidden = nn(head_t, grad_t)

    for copy in mates:
        copy.wait_recv()
    weights = w_all[...].reshape(parts * 2 * width, hid).astype(F32).T.astype(BF16)
    for copy in own_copies:
        copy.wait_recv()
    for copy in agg_copies:
        copy.wait_recv()
    x = x_all[...].reshape(parts * 2 * width, targets)
    preact = nn(weights, x)
    sigma = 1.0 / (1.0 + jnp.exp(-preact))
    hidden = (preact * sigma).astype(BF16)
    head_part[...] = nt(grad_t, hidden).reshape(head_part.shape)
    head_pair = pair_copy(0, head_part.at[:, mate], head_sib)
    head_pair.start()
    grad_pre = (grad_hidden * sigma * (1.0 + preact * (1.0 - sigma))).astype(BF16)
    grads = nt(x, grad_pre).reshape(g_part.shape)
    g_part[...] = grads
    g_pair = pair_copy(1, g_part.at[:, mate], g_sib)
    g_pair.start()

    head_pair.wait_recv()
    hrs = []
    for step in range(1, chips):
        to = lax.rem(chip + step, chips)
        head_send[step] = head_part[to, core] + head_sib[to]
        copy = chip_copy(step, head_send.at[step], head_recv.at[step], hrs_sems)
        copy.start()
        hrs.append(copy)
    g_pair.wait_recv()
    grs = []
    for step in range(1, chips):
        to = lax.rem(chip + step, chips)
        g_send[step] = (g_part[to, core] + g_sib[to]).astype(BF16)
        copy = chip_copy(step, g_send.at[step], g_recv.at[step], grs_sems)
        copy.start()
        grs.append(copy)
    scores_ref[...] = nn(wh_ref[...], hidden).T.astype(BF16)

    total = head_part[chip, core] + head_sib[chip]
    for step, copy in enumerate(hrs, 1):
        copy.wait_recv()
        total += head_recv[step]
    head_node[my_node] = total
    hns = []
    for step in range(1, nodes):
        copy = node_copy(step, head_node.at[my_node], head_node.at[my_node], hn_sems)
        copy.start()
        hns.append(copy)

    total = g_part[chip, core] + g_sib[chip]
    for step, copy in enumerate(grs, 1):
        copy.wait_recv()
        total += g_recv[step].astype(F32)
    g_node[my_node] = total.astype(BF16)
    gns = []
    for step in range(1, nodes):
        copy = node_copy(step, g_node.at[my_node], g_node.at[my_node], gn_sems)
        copy.start()
        gns.append(copy)

    for copy in hns:
        copy.wait_recv()
    total = head_node[0]
    for node in range(1, nodes):
        total += head_node[node]
    head_all[me] = total
    hags = []
    for step in range(1, parts):
        copy = feat_copy(step, head_all.at[me], head_all.at[me], hag_sems)
        copy.start()
        hags.append(copy)

    for copy in gns:
        copy.wait_recv()
    total = g_node[0].astype(F32)
    for node in range(1, nodes):
        total += g_node[node].astype(F32)
    grads_ref[...] = total

    for copy in hags:
        copy.wait_recv()
    head_ref[...] = head_all[...].reshape(head_ref.shape)
    for copy in (*w_copies, *mates, head_pair, g_pair, *own_copies, *agg_copies, *hrs, *grs, *hns, *gns, *hags):
        copy.wait_send()


def main_call(parts, nodes, inv, near, adj, own, wt, w_head, grad_scores):
    width = near.shape[1]
    targets, out = grad_scores.shape
    hid = w_head.shape[1]
    vmem = pl.BlockSpec(memory_space=pltpu.VMEM)
    anywhere = pl.BlockSpec(memory_space=pl.ANY)
    head_rows = out // parts
    feat_sems = pltpu.SemaphoreType.DMA((2, parts))
    chips = parts // 2
    chip_sems = pltpu.SemaphoreType.DMA((2, chips))
    node_sems = pltpu.SemaphoreType.DMA((2, nodes))
    return pl.pallas_call(
        functools.partial(main_kernel, parts, nodes),
        out_shape=(
            jax.ShapeDtypeStruct((targets, out), BF16),
            jax.ShapeDtypeStruct((2 * width, hid), F32),
            jax.ShapeDtypeStruct((out, hid), F32),
        ),
        in_specs=[vmem, anywhere, anywhere] + [vmem] * 4,
        out_specs=(vmem, vmem, vmem),
        scratch_shapes=[
            pltpu.VMEM(near.shape, BF16),
            pltpu.VMEM(adj.shape, BF16),
            pltpu.VMEM((parts, 2 * width, targets), BF16),
            pltpu.VMEM((chips, 2, 2 * width, hid), BF16),
            pltpu.VMEM((parts, width, targets), BF16),
            pltpu.VMEM((chips, 2, head_rows, hid), F32),
            pltpu.VMEM((chips, head_rows, hid), F32),
            pltpu.VMEM((chips, head_rows, hid), F32),
            pltpu.VMEM((chips, head_rows, hid), F32),
            pltpu.VMEM((nodes, head_rows, hid), F32),
            pltpu.VMEM((parts, head_rows, hid), F32),
            pltpu.VMEM((chips, 2, 2 * width, hid), F32),
            pltpu.VMEM((chips, 2 * width, hid), F32),
            pltpu.VMEM((chips, 2 * width, hid), BF16),
            pltpu.VMEM((chips, 2 * width, hid), BF16),
            pltpu.VMEM((nodes, 2 * width, hid), BF16),
            chip_sems, chip_sems, pltpu.SemaphoreType.DMA((2, 2)), feat_sems, feat_sems, chip_sems, chip_sems, node_sems, node_sems, feat_sems,
            pltpu.SemaphoreType.DMA((2, parts)),
        ],
        compiler_params=pltpu.CompilerParams(
            collective_id=0, has_side_effects=True, vmem_limit_bytes=VMEM_BYTES
        ),
        name="train_step",
    )(inv, near, adj, own, wt, w_head, grad_scores)


def hand_over_kernel(scores_in, head_in, grads_in, scores_ref, head_ref, neigh_ref, self_ref):
    width = neigh_ref.shape[0]
    scores_ref[...] = scores_in[...]
    head_ref[...] = head_in[...]
    neigh_ref[...] = grads_in[:width, :]
    self_ref[...] = grads_in[width:, :]


def hand_over(scores, head, grads):
    vmem = pl.BlockSpec(memory_space=pltpu.VMEM)
    half = jax.ShapeDtypeStruct((grads.shape[0] // 2, grads.shape[1]), F32)
    return pl.pallas_call(
        hand_over_kernel,
        out_shape=(
            jax.ShapeDtypeStruct(scores.shape, BF16), jax.ShapeDtypeStruct(head.shape, F32), half, half,
        ),
        in_specs=[vmem] * 3,
        out_specs=(vmem,) * 4,
        name="hand_over",
    )(scores, head, grads)


def solution(mesh):
    parts, nodes = mesh.shape["feat"], mesh.shape["node"]

    def body(
        features, target_ids, block_ids, tile_counts, adjacency, w_neigh, w_self, w_head, grad_scores
    ):
        feat = features[0]
        counts = tile_counts[0]
        own, near, wt, inv = gather_own(
            target_ids[0], block_ids[0].T, counts, feat, w_neigh.T, w_self.T, parts
        )
        scores, grads, head = main_call(
            parts, nodes, inv, near, adjacency[0], own, wt, w_head, grad_scores[0]
        )
        scores, head, neigh, own_grad = hand_over(scores, head, grads)
        return scores[None], head, neigh.T, own_grad.T

    in_specs = (
        P("node", "feat", None),
        P("node", None),
        P("node", None, None),
        P("node", None),
        P("node", None, None, None, None),
        P(None, "feat"),
        P(None, "feat"),
        P(),
        P("node", "feat", None),
    )
    out_specs = (P("node", "feat", None), P(), P(None, "feat"), P(None, "feat"))
    return jax.shard_map(body, mesh=mesh, in_specs=in_specs, out_specs=out_specs, check_vma=False)
```
